256 devices in a mesh: tm: 8 (over z), row: 8 (over x, y_hi), col: 4 (over y_lo, core).
Axes of the slice: x: 4, y: 4 (y_hi: 2, y_lo: 2; y = y_hi * 2 + y_lo), z: 8, core: 2. Of those that a mesh axis runs over, the one named last changes fastest.
Arguments:
- slopes: bfloat16 [2048, 40960], P('tm', 'col'), may hold values from -6 to 6
- reconstructor: bfloat16 [40960, 2048], P('col', 'row'), may hold values from -0.03125 to 0.03125
Outputs:
- moments: float32 [6, 2048, 6, 2048], P(None, ('tm', 'row'), None, 'col')
The draws below stay inside these ranges and needn't reach their ends.
All inputs are finite; a program needn't handle non-finite values.
Results may differ from the reference program's by a relative error of at most 0.0038.
Values may be sent and summed in bfloat16 or wider, within the bound.
A program may use at most 128 MiB of HBM per device.

```python
import jax
import jax.numpy as jnp

S = 40960
M = 2048
HIST = 5
FRAMES = 2048


def block_scale(stream_key, extent, shards, low, largest):
    def one(dim, blocks):
        draws = jax.random.uniform(jax.random.fold_in(jax.random.fold_in(stream_key, 6), dim), (blocks,), jnp.float32, low / len(shards), largest / len(shards))
        return jnp.repeat(jnp.exp(draws), extent[dim] // blocks).reshape((-1,) + (1,) * (len(extent) - dim - 1))

    gain = one(*shards[0])
    for cut in shards[1:]:
        gain = gain * one(*cut)
    return gain


def noise(rng, shape, width, limit, pieces=(), kind=jnp.bfloat16):
    level = block_scale(rng, shape, pieces, -0.22, 0.18) if pieces else 1.0
    drawn = jax.random.normal(rng, shape, jnp.float32) * width * level
    return jnp.minimum(jnp.maximum(drawn, -limit), limit).astype(kind)


def setup_inputs(seed: int = 0) -> dict:
    arg_keys = jax.random.split(jax.random.key(seed), 3)
    return {
        "slopes": noise(arg_keys[0], (FRAMES, S), 1.0, 6.0, ((0, 8), (1, 4))),
        "reconstructor": noise(arg_keys[1], (S, M), S ** -0.5, 0.03125, ((0, 4), (1, 8))),
    }


def reference(slopes, reconstructor):
    modes = jnp.dot(slopes, reconstructor, preferred_element_type=jnp.float32).astype(jnp.bfloat16)
    padded = jnp.concatenate([jnp.zeros((HIST, M), jnp.bfloat16), modes], axis=0)
    stacked = jnp.stack([padded[HIST - lag:HIST - lag + FRAMES] for lag in range(HIST + 1)], axis=1)
    history = stacked.reshape(FRAMES, (HIST + 1) * M)
    gram = jnp.dot(history.T, history, preferred_element_type=jnp.float32)
    gram = gram * (jnp.float32(FRAMES) ** -0.5)
    return gram.reshape(HIST + 1, M, HIST + 1, M)
```

```python
import functools

import jax
import jax.numpy as jnp
from jax import lax
from jax.experimental import pallas as pl
from jax.experimental.pallas import tpu as pltpu
from jax.sharding import PartitionSpec as P

MESH = pl.DeviceIdType.MESH
HIST = 5
LAGS = HIST + 1
SHIFTS = 2 * HIST + 1
NZ, NX, NC = 8, 4, 4
CHUNK = 1024


def gather_kernel(
    slopes_hbm, recon_hbm, sums, a_edge, g_edge,
    slopes, recon, part, inbox, modes, slab, left,
    load_sem, red_s, red_r, y_s, y_r, slab_s, slab_r, sib_s, sib_r,
    x_s, x_r, az_s, az_r, bz_s, bz_r, bx_s, bx_r,
):
    z = lax.axis_index("tm")
    row = lax.axis_index("row")
    c = lax.axis_index("col")
    x, yh = row // 2, row % 2
    yl, core = c // 2, c % 2
    depth = slopes_hbm.shape[1]
    chunks = depth // CHUNK

    def at(z_, x_, yh_, c_):
        return (z_, x_ * 2 + yh_, c_)

    loads = []
    for i in range(chunks):
        span = pl.ds(i * CHUNK, CHUNK)
        loads.append((
            pltpu.make_async_copy(slopes_hbm.at[:, span], slopes.at[:, span], load_sem.at[0, i]),
            pltpu.make_async_copy(recon_hbm.at[span], recon.at[span], load_sem.at[1, i]),
        ))
    for pair in loads:
        for copy in pair:
            copy.start()

    self_red = x == c
    self_slab = z == 2 * c + yh
    role = core == (z // 2) % 2
    slab_src_c, slab_src_yh = z // 2, z % 2

    barrier = pltpu.get_barrier_semaphore()

    def greet(device):
        pl.semaphore_signal(barrier, inc=1, device_id=device, device_id_type=MESH)

    for s in range(NC):
        @pl.when(jnp.logical_not(jnp.logical_and(self_red, c == s)))
        def _():
            greet(at(z, c, yh, s))
    greet(at(z, x, 1 - yh, c))
    for dx in (1, 2, 3):
        greet(at(z, (x + dx) % NX, yh, c))
    greet(at((z + 1) % NZ, x, yh, c))
    greet(at((z + NZ - 1) % NZ, x, yh, c))
    for s in range(NZ):
        @pl.when(jnp.logical_and(role, jnp.logical_not(jnp.logical_and(self_slab, z == s))))
        def _():
            greet(at(s, x, slab_src_yh, slab_src_c))

    @pl.when(jnp.logical_not(role))
    def _():
        greet(at(z, x, yh, 2 * yl + 1 - core))

    total = jnp.zeros((slopes.shape[0], recon.shape[1]), jnp.float32)
    for i in range(chunks):
        for copy in loads[i]:
            copy.wait()
        total += jnp.dot(
            slopes[:, i * CHUNK : (i + 1) * CHUNK],
            recon[i * CHUNK : (i + 1) * CHUNK, :],
            preferred_element_type=jnp.float32,
        )
    part[...] = total.T.reshape(part.shape)

    expected = (
        14
        - self_red.astype(jnp.int32)
        - self_slab.astype(jnp.int32)
        + role.astype(jnp.int32)
    )
    pl.semaphore_wait(barrier, expected)

    def red_copy(k, slot):
        return pltpu.make_async_remote_copy(
            src_ref=part.at[k], dst_ref=inbox.at[slot], send_sem=red_s.at[k], recv_sem=red_r.at[slot],
            device_id=at(z, k, yh, x), device_id_type=MESH,
        )

    for k in range(NX):
        here = jnp.logical_and(self_red, x == k)

        @pl.when(jnp.logical_not(here))
        def _():
            red_copy(k, c).start()

        @pl.when(here)
        def _():
            inbox[k] = part[k]

    for s in range(NC):
        @pl.when(jnp.logical_not(jnp.logical_and(self_red, c == s)))
        def _():
            red_copy(0, s).wait_recv()

    own = (inbox[0] + inbox[1]) + (inbox[2] + inbox[3])
    modes[z, yh, x] = own.astype(jnp.bfloat16).reshape(modes.shape[3:])

    def remote(ref, send, recv, device):
        return pltpu.make_async_remote_copy(
            src_ref=ref, dst_ref=ref, send_sem=send, recv_sem=recv, device_id=device, device_id_type=MESH
        )

    zs = [(z + j) % NZ for j in range(NZ)]
    yhs = (yh, 1 - yh)
    up, down = at(zs[1], x, yh, c), at(zs[7], x, yh, c)
    sent = []

    def start(copy):
        copy.start()
        sent.append(copy)

    def x_peer(d):
        return at(z, (x + d) % NX, yh, c)

    def own_x(s, d):
        return remote(modes.at[z, yhs[s], x], x_s.at[s, d - 1], x_r.at[s, d - 1], x_peer(d))

    def b_x(s, j, d):
        return remote(modes.at[zs[j], yhs[s], x, 1], bx_s.at[s, j, d - 1], bx_r.at[s, j, d - 1], x_peer(d))

    def b_z(s, j, way):
        origin = zs[(NZ - j + 1) % NZ] if way == 0 else zs[j - 1]
        ref = modes.at[origin, yhs[s], x, 1]
        if j == 4:
            ref = ref.at[pl.ds(16 * way, 16)]
        return remote(ref, bz_s.at[s, way, j - 1], bz_r.at[s, way, j - 1], up if way == 0 else down)

    def a_z(s, j, way):
        origin = zs[(NZ - j + 1) % NZ] if way == 0 else zs[j - 1]
        ref = modes.at[origin, yhs[s], pl.ds(2 * way, 2) if j == 4 else pl.ds(0, 4), 0]
        return remote(ref, az_s.at[s, way, j - 1], az_r.at[s, way, j - 1], up if way == 0 else down)

    y_copy = remote(modes.at[z, yh, x], y_s.at[0], y_r.at[0], at(z, x, 1 - yh, c))
    start(y_copy)

    def begin(s):
        for d in (1, 3, 2):
            start(own_x(s, d))
        for way in range(2):
            start(b_z(s, 1, way))

    begin(0)

    def slab_copy(h, yl_, slot):
        return pltpu.make_async_remote_copy(
            src_ref=modes.at[z, yh, x, h], dst_ref=slab.at[slot], send_sem=slab_s.at[h, yl_],
            recv_sem=slab_r.at[slot], device_id=at(2 * c + yh, x, h, 2 * yl_ + core), device_id_type=MESH,
        )

    for h in range(2):
        for yl_ in range(2):
            here = jnp.logical_and(self_slab, jnp.logical_and(yh == h, yl == yl_))

            @pl.when(jnp.logical_not(here))
            def _():
                slab_copy(h, yl_, z).start()

            @pl.when(here)
            def _():
                slab[z] = modes[z, yh, x, h]

    y_copy.wait_recv()
    begin(1)

    def b_step(s, j):
        for way in range(2):
            b_z(s, j, way).wait_recv()
            if j < 4:
                start(b_z(s, j + 1, way))
        if j < 4:
            for d in (1, 3, 2):
                start(b_x(s, NZ - j, d))
                start(b_x(s, j, d))
        else:
            for d in (1, 3, 2):
                start(b_x(s, 4, d))

    def a_step(s, j):
        if j == 0:
            for d in (1, 3, 2):
                own_x(s, d).wait_recv()
            for way in range(2):
                start(a_z(s, 1, way))
        else:
            for way in range(2):
                a_z(s, j, way).wait_recv()
                if j < 4:
                    start(a_z(s, j + 1, way))

    sibling = remote(slab, sib_s.at[0], sib_r.at[0], at(z, x, yh, 2 * yl + 1 - core))
    for j in range(1, 5):
        for s in range(2):
            b_step(s, j)
            a_step(s, j - 1)
        if j == 2:
            @pl.when(role)
            def _():
                for s in range(NZ):
                    @pl.when(jnp.logical_not(jnp.logical_and(self_slab, z == s)))
                    def _():
                        slab_copy(0, 0, s).wait_recv()
                sibling.start()

    @pl.when(jnp.logical_not(role))
    def _():
        sibling.wait_recv()

    rows = slab.shape[1]
    wide = slab.shape[2]
    frames = NZ * wide
    edge = jnp.zeros((rows, 128), jnp.float32)
    line = jnp.concatenate([edge] + [slab[i].astype(jnp.float32) for i in range(NZ)] + [edge], axis=1)
    span = frames + 256
    lane = lax.broadcasted_iota(jnp.int32, (rows, wide), 1)
    for i in range(SHIFTS):
        d = i - HIST
        moved = line if d == 0 else pltpu.roll(line, (span - d) % span, 1)
        for q in range(NZ):
            piece = moved[:, 128 + q * wide : 128 + (q + 1) * wide]
            if q == NZ - 1:
                piece = jnp.where(lane <= wide - 1 - HIST + max(0, -d), piece, 0.0)
            left[q, i * rows : (i + 1) * rows, :] = piece.astype(jnp.bfloat16)
    a_edge[...] = line[:, frames : frames + 128]

    for s in range(2):
        a_step(s, 4)
    for s in range(2):
        for j in range(1, NZ):
            for d in (1, 2, 3):
                b_x(s, j, d).wait_recv()

    def block(q):
        return modes[q].reshape(2 * 4 * 2 * 32, wide)

    def dot(q):
        return lax.dot_general(
            left[q], block(q), (((1,), (1,)), ((), ())), preferred_element_type=jnp.float32
        )

    acc = dot(0)
    for q in range(1, NZ):
        acc += dot(q)
    sums[...] = acc.reshape(sums.shape)
    tail = block(NZ - 1)[:, wide - 128 :].astype(jnp.float32)
    g_edge[...] = tail.T[120:128, :]

    for copy in sent:
        copy.wait_send()
    for k in range(NX):
        @pl.when(jnp.logical_not(jnp.logical_and(self_red, x == k)))
        def _():
            red_copy(k, c).wait_send()
    for h in range(2):
        for yl_ in range(2):
            here = jnp.logical_and(self_slab, jnp.logical_and(yh == h, yl == yl_))

            @pl.when(jnp.logical_not(here))
            def _():
                slab_copy(h, yl_, z).wait_send()

    @pl.when(role)
    def _():
        sibling.wait_send()


def spread_kernel(scale, sums, a_edge, g_edge, out):
    for i in range(SHIFTS):
        d = i - HIST
        l1, l2 = (HIST - d, HIST) if d >= 0 else (HIST, HIST + d)
        value = sums[i]
        while True:
            out[l1, l2] = value * scale
            if min(l1, l2) == 0:
                break
            l1, l2 = l1 - 1, l2 - 1
            value = value + a_edge[:, 127 - l1 : 128 - l1] * g_edge[7 - l2 : 8 - l2, :]


def local(slopes, reconstructor):
    frames_dev, depth = slopes.shape
    block = reconstructor.shape[1]
    frames = frames_dev * NZ
    width = 2 * block
    rows = 32
    piece = block // NX
    vmem = pl.BlockSpec(memory_space=pltpu.VMEM)
    hbm = pl.BlockSpec(memory_space=pl.ANY)
    dma = pltpu.SemaphoreType.DMA
    sums, a_edge, g_edge = pl.pallas_call(
        gather_kernel,
        out_shape=[
            jax.ShapeDtypeStruct((SHIFTS, rows, width), jnp.float32),
            jax.ShapeDtypeStruct((rows, 128), jnp.float32),
            jax.ShapeDtypeStruct((8, width), jnp.float32),
        ],
        in_specs=[hbm, hbm],
        out_specs=[vmem, vmem, vmem],
        scratch_shapes=[
            pltpu.VMEM((frames_dev, depth), jnp.bfloat16),
            pltpu.VMEM((depth, block), jnp.bfloat16),
            pltpu.VMEM((NX, piece, frames_dev), jnp.float32),
            pltpu.VMEM((NC, piece, frames_dev), jnp.float32),
            pltpu.VMEM((NZ, 2, NX, 2, rows, frames_dev), jnp.bfloat16),
            pltpu.VMEM((NZ, rows, frames_dev), jnp.bfloat16),
            pltpu.VMEM((NZ, SHIFTS * rows, frames_dev), jnp.bfloat16),
            dma((2, depth // CHUNK)),
            dma((NX,)), dma((NC,)),
            dma((1,)), dma((1,)),
            dma((2, 2)), dma((NZ,)),
            dma((1,)), dma((1,)),
            dma((2, 3)), dma((2, 3)),
            dma((2, 2, 4)), dma((2, 2, 4)),
            dma((2, 2, 4)), dma((2, 2, 4)),
            dma((2, NZ, 3)), dma((2, NZ, 3)),
        ],
        compiler_params=pltpu.CompilerParams(
            collective_id=0, has_side_effects=True, vmem_limit_bytes=48 * 2**20
        ),
        name="gather",
    )(slopes, reconstructor)
    scale = float(frames) ** -0.5
    steps = 4
    sub = rows // steps
    out = pl.pallas_call(
        functools.partial(spread_kernel, scale),
        grid=(steps,),
        out_shape=jax.ShapeDtypeStruct((LAGS, LAGS, rows, width), jnp.float32),
        in_specs=[
            pl.BlockSpec((SHIFTS, sub, width), lambda i: (0, i, 0)),
            pl.BlockSpec((sub, 128), lambda i: (i, 0)),
            pl.BlockSpec((8, width), lambda i: (0, 0)),
        ],
        out_specs=pl.BlockSpec((LAGS, LAGS, sub, width), lambda i: (0, 0, i, 0)),
        name="spread",
    )(sums, a_edge, g_edge)
    return out.transpose(0, 2, 1, 3)


def solution(mesh):
    return jax.shard_map(
        local,
        mesh=mesh,
        in_specs=(P("tm", "col"), P("col", "row")),
        out_specs=P(None, ("tm", "row"), None, "col"),
        check_vma=False,
    )
```

```python
import functools

import jax
import jax.numpy as jnp
from jax import lax
from jax.experimental import pallas as pl
from jax.experimental.pallas import tpu as pltpu
from jax.sharding import PartitionSpec as P

MESH = pl.DeviceIdType.MESH
HIST = 5
LAGS = HIST + 1
SHIFTS = 2 * HIST + 1
NZ, NX, NC = 8, 4, 4
CHUNK = 1024


def gather_kernel(
    slopes_hbm, recon_hbm, sums, a_edge, g_edge,
    slopes, recon, part, inbox, modes, slab, left,
    load_sem, red_s, red_r, slab_s, slab_r, fan_s, fan_r,
    push_s, push_r, oz_s, oz_r, bz_s, bz_r, az_s, az_r, bx_s, bx_r, yl_s, yl_r,
):
    z = lax.axis_index("tm")
    row = lax.axis_index("row")
    c = lax.axis_index("col")
    x, yh = row // 2, row % 2
    yl, core = c // 2, c % 2
    depth = slopes_hbm.shape[1]
    chunks = depth // CHUNK

    def at(z_, x_, yh_, c_):
        return (z_, x_ * 2 + yh_, c_)

    loads = []
    for i in range(chunks):
        span = pl.ds(i * CHUNK, CHUNK)
        loads.append((
            pltpu.make_async_copy(slopes_hbm.at[:, span], slopes.at[:, span], load_sem.at[0, i]),
            pltpu.make_async_copy(recon_hbm.at[span], recon.at[span], load_sem.at[1, i]),
        ))
    for pair in loads:
        for copy in pair:
            copy.start()

    self_red = x == c
    self_slab = z == 2 * c + yh
    role = c == z // 2
    zs = [(z + j) % NZ for j in range(NZ)]
    xs = [(x + j) % NX for j in range(NX)]
    yhs = (yh, 1 - yh)
    fan = [at(z, x, yh, 2 * yl + 1 - core), at(z, x, yh, 2 * (1 - yl) + core), at(z, x, yh, 3 - c)]

    def z_peer(way, dist, s=0):
        return at(zs[dist] if way == 0 else zs[NZ - dist], x, yhs[s], c)

    def x_peer(d, s=0):
        return at(z, xs[d], yhs[s], c)

    pushes = [(0, 1), (0, 3), (0, 2), (1, 0), (1, 1), (1, 3), (1, 2)]

    barrier = pltpu.get_barrier_semaphore()

    def greet(device):
        pl.semaphore_signal(barrier, inc=1, device_id=device, device_id_type=MESH)

    for s in range(NC):
        @pl.when(jnp.logical_not(jnp.logical_and(self_red, c == s)))
        def _():
            greet(at(z, c, yh, s))
    for s, d in pushes:
        greet(x_peer(d, s))
    for way in range(2):
        for dist in (1, 2):
            for s in range(2):
                greet(z_peer(way, dist, s))
    for s in range(NZ):
        @pl.when(jnp.logical_and(role, jnp.logical_not(jnp.logical_and(self_slab, z == s))))
        def _():
            greet(at(s, x, z % 2, c))

    @pl.when(jnp.logical_not(role))
    def _():
        greet(at(z, x, yh, z // 2))

    total = jnp.zeros((slopes.shape[0], recon.shape[1]), jnp.float32)
    for i in range(chunks):
        for copy in loads[i]:
            copy.wait()
        total += jnp.dot(
            slopes[:, i * CHUNK : (i + 1) * CHUNK],
            recon[i * CHUNK : (i + 1) * CHUNK, :],
            preferred_element_type=jnp.float32,
        )
    part[...] = total.T.reshape(part.shape)

    expected = (
        21
        - self_red.astype(jnp.int32)
        - self_slab.astype(jnp.int32)
        + 3 * role.astype(jnp.int32)
    )
    pl.semaphore_wait(barrier, expected)

    def red_copy(k, slot):
        return pltpu.make_async_remote_copy(
            src_ref=part.at[k], dst_ref=inbox.at[slot], send_sem=red_s.at[k], recv_sem=red_r.at[slot],
            device_id=at(z, k, yh, x), device_id_type=MESH,
        )

    for k in range(NX):
        here = jnp.logical_and(self_red, x == k)

        @pl.when(jnp.logical_not(here))
        def _():
            red_copy(k, c).start()

        @pl.when(here)
        def _():
            inbox[k] = part[k]

    for s in range(NC):
        @pl.when(jnp.logical_not(jnp.logical_and(self_red, c == s)))
        def _():
            red_copy(0, s).wait_recv()

    own = (inbox[0] + inbox[1]) + (inbox[2] + inbox[3])
    modes[z, 0, 0] = own.astype(jnp.bfloat16).reshape(modes.shape[3:])

    def remote(src, dst, send, recv, device):
        return pltpu.make_async_remote_copy(
            src_ref=src, dst_ref=dst, send_sem=send, recv_sem=recv, device_id=device, device_id_type=MESH
        )

    sent = [[]]

    def start(copy):
        copy.start()
        sent[-1].append(copy)

    def settle():
        for copy in sent.pop(0):
            copy.wait_send()

    slot_of = (0, 1, 3, 2)
    groups = (pl.ds(0, 1), pl.ds(1, 2), pl.ds(3, 1))

    def origin(j, way):
        return zs[(NZ - j + 1) % NZ] if way == 0 else zs[j - 1]

    def push(s, d):
        slot = slot_of[(NX - d) % NX]
        return remote(
            modes.at[z, 0, 0], modes.at[z, s, slot], push_s.at[s, slot], push_r.at[s, slot], x_peer(d, s)
        )

    def pushed(s, slot):
        return remote(modes.at[z, s, slot], modes.at[z, s, slot], push_s.at[s, slot], push_r.at[s, slot], x_peer(1))

    def own_z(way):
        ref = modes.at[origin(1, way), 0, 0]
        return remote(ref, ref, oz_s.at[way], oz_r.at[way], z_peer(way, 1))

    def b_z(s, way, dist):
        far = dist > 2
        ref = modes.at[origin(3 if far else 1, way), s, 0, 1]
        src = ref if far else modes.at[z, 0, 0, 1]
        return remote(
            src, ref, bz_s.at[s, way, dist - 1], bz_r.at[s, way, dist - 1],
            z_peer(way, dist - 2, 0) if far else z_peer(way, dist, s),
        )

    def a_z(s, j, way, g):
        span = groups[g]
        if j == 4 and g == 1:
            span = pl.ds(1 + way, 1)
        ref = modes.at[origin(j, way), s, span, 0]
        if s == 1:
            ref = ref.at[:, pl.ds(0, 16)]
        return remote(ref, ref, az_s.at[s, way, j - 1, g], az_r.at[s, way, j - 1, g], z_peer(way, 1))

    def last(j, way, g):
        return j < 4 or g == 1 or (g == 0) == (way == 0)

    def b_x(s, j, d):
        src = modes.at[zs[j], s, 0, 1]
        dst = modes.at[zs[j], s, slot_of[(NX - d) % NX], 1]
        return remote(src, dst, bx_s.at[s, j, d - 1], bx_r.at[s, j, d - 1], x_peer(d))

    def y_last(j, g, way):
        span, slot = groups[g], g
        if j == 4 and g == 1:
            span = pl.ds(1 + way, 1)
            slot = 3 if way == 1 else 1
        src = modes.at[zs[j], 0, span, 0, pl.ds(16, 16)]
        dst = modes.at[zs[j], 1, span, 0, pl.ds(16, 16)]
        return remote(src, dst, yl_s.at[j, slot], yl_r.at[j, slot], x_peer(0, 1))

    near = (1, 3, 2)

    def send_bx(s, j):
        for d in near:
            start(b_x(s, j, d))

    def take_own():
        for way in range(2):
            own_z(way).wait_recv()
            start(a_z(0, 2, way, 0))
        for way in range(2):
            start(y_last((7, 1)[way], 0, way))
            send_bx(0, (7, 1)[way])

    def take_push(s, g):
        for slot in ((0,), (1, 2), (3,))[g]:
            pushed(s, slot).wait_recv()
        for way in range(2):
            start(a_z(s, 1, way, g))

    def take_b(s, dist):
        for way in range(2):
            if dist == 4 and s != way:
                continue
            b_z(s, way, dist).wait_recv()
            if dist == 2:
                start(b_z(s, way, 3))
                if s == way:
                    start(b_z(s, way, 4))
            send_bx(s, (NZ - dist, dist)[way])

    def take_a(s, j, g):
        for way in range(2):
            if not last(j, way, g):
                continue
            a_z(s, j, way, g).wait_recv()
            if j < 4 and last(j + 1, way, g):
                start(a_z(s, j + 1, way, g))
            if s == 0:
                start(y_last((NZ - j, j)[way], g, way))

    def take_bx(j):
        for s in range(2):
            for q in sorted({j, NZ - j}):
                for d in near:
                    b_x(s, q, d).wait_recv()

    def take_yl(j):
        for q in sorted({j, NZ - j}):
            for g in range(3):
                y_last(q, g, 0).wait_recv()
                if j == 4 and g == 1:
                    y_last(q, g, 1).wait_recv()

    def slab_copy(h, slot):
        return pltpu.make_async_remote_copy(
            src_ref=modes.at[z, 0, 0, h], dst_ref=slab.at[slot], send_sem=slab_s.at[h],
            recv_sem=slab_r.at[slot], device_id=at(2 * c + yh, x, h, c), device_id_type=MESH,
        )

    def fan_copy(i):
        return remote(slab, slab, fan_s.at[i], fan_r.at[0], fan[i])

    for way in range(2):
        start(own_z(way))
    start(push(0, 1))
    start(push(0, 3))
    for way in range(2):
        start(b_z(0, way, 2))
    start(push(0, 2))
    start(push(1, 0))
    for dist in (1, 2):
        for way in range(2):
            start(b_z(1, way, dist))
    for d in near:
        start(push(1, d))
    for h in range(2):
        here = jnp.logical_and(self_slab, yh == h)

        @pl.when(jnp.logical_not(here))
        def _():
            slab_copy(h, z).start()

        @pl.when(here)
        def _():
            slab[z] = modes[z, 0, 0, h]

    sent.append([])
    take_own()
    take_push(0, 1)
    take_push(0, 2)
    take_b(0, 2)
    take_push(1, 0)
    take_b(1, 1)
    take_push(1, 1)
    take_push(1, 2)
    take_b(1, 2)
    sent.append([])
    for g in (1, 2):
        take_a(0, 1, g)
    for g in range(3):
        take_a(1, 1, g)
    settle()
    take_a(0, 2, 0)

    @pl.when(role)
    def _():
        for s in range(NZ):
            @pl.when(jnp.logical_not(jnp.logical_and(self_slab, z == s)))
            def _():
                slab_copy(0, s).wait_recv()
        for i in range(3):
            fan_copy(i).start()

    take_b(0, 3)
    take_b(1, 3)
    for g in (1, 2):
        take_a(0, 2, g)
    take_b(0, 4)
    take_b(1, 4)
    for g in range(3):
        take_a(1, 2, g)
    settle()
    sent.append([])
    for g in range(3):
        take_a(0, 3, g)
    for g in range(3):
        take_a(1, 3, g)
    settle()

    @pl.when(jnp.logical_not(role))
    def _():
        fan_copy(0).wait_recv()

    rows = slab.shape[1]
    wide = slab.shape[2]
    frames = NZ * wide
    edge = jnp.zeros((rows, 128), jnp.float32)
    line = jnp.concatenate([edge] + [slab[i].astype(jnp.float32) for i in range(NZ)] + [edge], axis=1)
    span = frames + 256
    lane = lax.broadcasted_iota(jnp.int32, (rows, wide), 1)
    for i in range(SHIFTS):
        d = i - HIST
        moved = line if d == 0 else pltpu.roll(line, (span - d) % span, 1)
        for q in range(NZ):
            piece = moved[:, 128 + q * wide : 128 + (q + 1) * wide]
            if q == NZ - 1:
                piece = jnp.where(lane <= wide - 1 - HIST + max(0, -d), piece, 0.0)
            left[q, i * rows : (i + 1) * rows, :] = piece.astype(jnp.bfloat16)
    a_edge[...] = line[:, frames : frames + 128]

    def block(q):
        pieces = []
        for yh_ in range(2):
            for x_ in range(NX):
                s = lax.rem(yh + yh_, 2)
                r = lax.rem(x_ - x + NX, NX)
                slot = r + (r == 2).astype(jnp.int32) - (r == 3).astype(jnp.int32)
                pieces.append(modes[q, s, slot].reshape(64, wide))
        return jnp.concatenate(pieces, axis=0)

    def dot(j):
        return lax.dot_general(
            left[zs[j]], block(zs[j]), (((1,), (1,)), ((), ())), preferred_element_type=jnp.float32
        ).reshape(sums.shape)

    take_bx(1)
    take_yl(1)
    sums[...] = dot(0) + dot(1) + dot(7)
    for g in range(3):
        take_a(0, 4, g)
    for g in range(3):
        take_a(1, 4, g)
    settle()
    take_bx(2)
    take_yl(2)
    sums[...] += dot(2) + dot(6)
    take_bx(3)
    take_yl(3)
    sums[...] += dot(3) + dot(5)
    take_bx(4)
    take_yl(4)
    sums[...] += dot(4)
    tail = block(NZ - 1)[:, wide - 128 :].astype(jnp.float32)
    g_edge[...] = tail.T[120:128, :]

    while sent:
        settle()
    for k in range(NX):
        @pl.when(jnp.logical_not(jnp.logical_and(self_red, x == k)))
        def _():
            red_copy(k, c).wait_send()
    for h in range(2):
        @pl.when(jnp.logical_not(jnp.logical_and(self_slab, yh == h)))
        def _():
            slab_copy(h, z).wait_send()

    @pl.when(role)
    def _():
        for i in range(3):
            fan_copy(i).wait_send()


def spread_kernel(scale, sums, a_edge, g_edge, out, stage, sem):
    copies = []
    for i in range(SHIFTS):
        d = i - HIST
        l1, l2 = (HIST - d, HIST) if d >= 0 else (HIST, HIST + d)
        value = sums[i]
        while True:
            stage[l1, l2] = value * scale
            copy = pltpu.make_async_copy(stage.at[l1, l2], out.at[l1, l2], sem.at[l1, l2])
            copy.start()
            copies.append(copy)
            if min(l1, l2) == 0:
                break
            l1, l2 = l1 - 1, l2 - 1
            value = value + a_edge[:, 127 - l1 : 128 - l1] * g_edge[7 - l2 : 8 - l2, :]
    for copy in copies:
        copy.wait()


def local(slopes, reconstructor):
    frames_dev, depth = slopes.shape
    block = reconstructor.shape[1]
    frames = frames_dev * NZ
    width = 2 * block
    rows = 32
    piece = block // NX
    vmem = pl.BlockSpec(memory_space=pltpu.VMEM)
    hbm = pl.BlockSpec(memory_space=pl.ANY)
    dma = pltpu.SemaphoreType.DMA
    sums, a_edge, g_edge = pl.pallas_call(
        gather_kernel,
        out_shape=[
            jax.ShapeDtypeStruct((SHIFTS, rows, width), jnp.float32),
            jax.ShapeDtypeStruct((rows, 128), jnp.float32),
            jax.ShapeDtypeStruct((8, width), jnp.float32),
        ],
        in_specs=[hbm, hbm],
        out_specs=[vmem, vmem, vmem],
        scratch_shapes=[
            pltpu.VMEM((frames_dev, depth), jnp.bfloat16),
            pltpu.VMEM((depth, block), jnp.bfloat16),
            pltpu.VMEM((NX, piece, frames_dev), jnp.float32),
            pltpu.VMEM((NC, piece, frames_dev), jnp.float32),
            pltpu.VMEM((NZ, 2, NX, 2, rows, frames_dev), jnp.bfloat16),
            pltpu.VMEM((NZ, rows, frames_dev), jnp.bfloat16),
            pltpu.VMEM((NZ, SHIFTS * rows, frames_dev), jnp.bfloat16),
            dma((2, depth // CHUNK)),
            dma((NX,)), dma((NC,)),
            dma((2,)), dma((NZ,)),
            dma((3,)), dma((1,)),
            dma((2, 4)), dma((2, 4)),
            dma((2,)), dma((2,)),
            dma((2, 2, 4)), dma((2, 2, 4)),
            dma((2, 2, 4, 3)), dma((2, 2, 4, 3)),
            dma((2, NZ, 3)), dma((2, NZ, 3)),
            dma((NZ, 4)), dma((NZ, 4)),
        ],
        compiler_params=pltpu.CompilerParams(
            collective_id=0, has_side_effects=True, vmem_limit_bytes=51 * 2**20
        ),
        name="gather",
    )(slopes, reconstructor)
    scale = float(frames) ** -0.5
    out = pl.pallas_call(
        functools.partial(spread_kernel, scale),
        out_shape=jax.ShapeDtypeStruct((LAGS, LAGS, rows, width), jnp.float32),
        in_specs=[vmem, vmem, vmem],
        out_specs=pl.BlockSpec(memory_space=pl.ANY),
        scratch_shapes=[pltpu.VMEM((LAGS, LAGS, rows, width), jnp.float32), dma((LAGS, LAGS))],
        compiler_params=pltpu.CompilerParams(vmem_limit_bytes=32 * 2**20),
        name="spread",
    )(sums, a_edge, g_edge)
    return out.transpose(0, 2, 1, 3)


def solution(mesh):
    return jax.shard_map(
        local,
        mesh=mesh,
        in_specs=(P("tm", "col"), P("col", "row")),
        out_specs=P(None, ("tm", "row"), None, "col"),
        check_vma=False,
    )
```

```python
import functools

import jax
import jax.numpy as jnp
from jax import lax
from jax.experimental import pallas as pl
from jax.experimental.pallas import tpu as pltpu
from jax.sharding import PartitionSpec as P

MESH = pl.DeviceIdType.MESH
HIST = 5
LAGS = HIST + 1
SHIFTS = 2 * HIST + 1
NZ, NX, NC = 8, 4, 4
CHUNK = 1024
EARLY = 16
GROUPS = ((0, 1, 32), (1, 2, 32), (3, 2, 16), (5, 3, 16))


def gather_kernel(
    slopes_hbm, recon_hbm, sums, a_edge, g_edge,
    slopes, recon, part, inbox, modes, slab, left,
    load_sem, red_s, red_r, slab_s, slab_r,
    xy_s, xy_r, z_s, z_r, xyz_s, xyz_r, x1_s, x1_r, y1_s, y1_r, x2_s, x2_r, y2_s, y2_r,
):
    z = lax.axis_index("tm")
    row = lax.axis_index("row")
    c = lax.axis_index("col")
    x, yh = row // 2, row % 2
    yl, core = c // 2, c % 2
    depth = slopes_hbm.shape[1]
    chunks = depth // CHUNK

    def at(z_, x_, yh_, c_):
        return (z_, x_ * 2 + yh_, c_)

    loads = []
    for i in range(chunks):
        span = pl.ds(i * CHUNK, CHUNK)
        loads.append((
            pltpu.make_async_copy(slopes_hbm.at[:, span], slopes.at[:, span], load_sem.at[0, i]),
            pltpu.make_async_copy(recon_hbm.at[span], recon.at[span], load_sem.at[1, i]),
        ))
    for pair in loads:
        for copy in pair:
            copy.start()

    self_red = x == c
    source = jnp.logical_and(c == z // 2, yh == z % 2)
    relay = jnp.logical_and(core == (z // 2) % 2, jnp.logical_not(source))
    leaf = core != (z // 2) % 2
    zs = [(z + j) % NZ for j in range(NZ)]
    xs = [(x + j) % NX for j in range(NX)]
    yhs = (yh, 1 - yh)
    sibling = at(z, x, yh, 2 * yl + 1 - core)

    z_order = (0, 1, 7, 2, 6, 3, 5, 4)
    xy_order = ((0, 1), (0, 3), (0, 2), (1, 0), (1, 1), (1, 3), (1, 2))

    def z_peer(j):
        return at(zs[j], x, yh, c)

    def xy_peer(s, d):
        return at(z, xs[d], yhs[s], c)

    barrier = pltpu.get_barrier_semaphore()

    def greet(device):
        pl.semaphore_signal(barrier, inc=1, device_id=device, device_id_type=MESH)

    for s in range(NC):
        @pl.when(jnp.logical_not(jnp.logical_and(self_red, c == s)))
        def _():
            greet(at(z, c, yh, s))
    for s, d in xy_order:
        greet(xy_peer(s, d))
    for j in (1, 7, 2, 6):
        greet(z_peer(j))

    @pl.when(relay)
    def _():
        greet(at(z, x, z % 2, z // 2))

    @pl.when(leaf)
    def _():
        greet(sibling)

    total = jnp.zeros((slopes.shape[0], recon.shape[1]), jnp.float32)
    for i in range(chunks):
        for copy in loads[i]:
            copy.wait()
        total += jnp.dot(
            slopes[:, i * CHUNK : (i + 1) * CHUNK],
            recon[i * CHUNK : (i + 1) * CHUNK, :],
            preferred_element_type=jnp.float32,
        )
    part[...] = total.T.reshape(part.shape)

    expected = (
        15
        - self_red.astype(jnp.int32)
        + 4 * source.astype(jnp.int32)
        + relay.astype(jnp.int32)
    )
    pl.semaphore_wait(barrier, expected)

    def red_copy(k, slot):
        return pltpu.make_async_remote_copy(
            src_ref=part.at[k], dst_ref=inbox.at[slot], send_sem=red_s.at[k], recv_sem=red_r.at[slot],
            device_id=at(z, k, yh, x), device_id_type=MESH,
        )

    for k in range(NX):
        here = jnp.logical_and(self_red, x == k)

        @pl.when(jnp.logical_not(here))
        def _():
            red_copy(k, c).start()

        @pl.when(here)
        def _():
            inbox[k] = part[k]

    for s in range(NC):
        @pl.when(jnp.logical_not(jnp.logical_and(self_red, c == s)))
        def _():
            red_copy(0, s).wait_recv()

    own = (inbox[0] + inbox[1]) + (inbox[2] + inbox[3])
    modes[0, 0, 0] = own.astype(jnp.bfloat16)

    def remote(src, dst, send, recv, device):
        return pltpu.make_async_remote_copy(
            src_ref=src, dst_ref=dst, send_sem=send, recv_sem=recv, device_id=device, device_id_type=MESH
        )

    sent = []

    def start(copy):
        copy.start()
        sent.append(copy)

    def x_slot(d):
        return (0, 1, 3, 2)[d % NX]

    def z_slot(j):
        return z_order.index(j % NZ)

    early, late = pl.ds(0, EARLY), pl.ds(EARLY, 64 - EARLY)

    def part_a(g):
        return pl.ds(EARLY, GROUPS[g][2])

    def part_b(g):
        return pl.ds(EARLY + GROUPS[g][2], 64 - EARLY - GROUPS[g][2])

    def z_span(g):
        return pl.ds(GROUPS[g][0], GROUPS[g][1])

    def xy_push(s, d):
        slot = x_slot(-d)
        return remote(
            modes.at[0, 0, 0, early], modes.at[0, s, slot, early], xy_s.at[s, slot], xy_r.at[s, slot], xy_peer(s, d)
        )

    def z_push(j):
        slot = z_slot(-j)
        return remote(modes.at[0, 0, 0], modes.at[slot, 0, 0], z_s.at[slot], z_r.at[slot], z_peer(j))

    def z_pass(j, hops):
        slot = z_slot(-j - hops)
        sem, rows_ = slot, pl.ds(0, 64)
        if abs(hops) == 2:
            sem, rows_ = (slot, pl.ds(0, 32)) if hops > 0 else (0, pl.ds(32, 32))
        return remote(
            modes.at[z_slot(-j), 0, 0, rows_], modes.at[slot, 0, 0, rows_], z_s.at[sem], z_r.at[sem],
            z_peer(hops % NZ),
        )

    def slots(s):
        return pl.ds(1 - s, NX - 1 + s)

    def xy_then_z(s, j):
        slot = z_slot(-j)
        return remote(
            modes.at[0, s, slots(s), early], modes.at[slot, s, slots(s), early], xyz_s.at[s, slot], xyz_r.at[s, slot],
            z_peer(j),
        )

    def pass_z(s, j, hops):
        slot = z_slot(-j - hops)
        return remote(
            modes.at[z_slot(-j), s, slots(s), early], modes.at[slot, s, slots(s), early],
            xyz_s.at[s, slot], xyz_r.at[s, slot], z_peer(hops % NZ),
        )

    def x_first(g, d):
        slot = x_slot(-d)
        return remote(
            modes.at[z_span(g), 0, 0, late], modes.at[z_span(g), 0, slot, late], x1_s.at[g, slot], x1_r.at[g, slot],
            xy_peer(0, d),
        )

    def y_first(g):
        return remote(
            modes.at[z_span(g), 0, 0, late], modes.at[z_span(g), 1, 0, late], y1_s.at[g], y1_r.at[g], xy_peer(1, 0)
        )

    def x_second(g, d):
        slot = x_slot(-d)
        return remote(
            modes.at[z_span(g), 1, 0, part_a(g)], modes.at[z_span(g), 1, slot, part_a(g)],
            x2_s.at[g, slot], x2_r.at[g, slot], xy_peer(0, d),
        )

    def y_second(g):
        span = pl.ds(1, NX - 1)
        return remote(
            modes.at[z_span(g), 0, span, part_b(g)], modes.at[z_span(g), 1, span, part_b(g)],
            y2_s.at[g], y2_r.at[g], xy_peer(1, 0),
        )

    def slab_copy(g, i):
        plane = yh if i < 2 else 1 - yh
        span = pl.ds(pl.multiple_of(32 * plane, 32), 32)
        other = 2 * (1 - yl) + core
        device = (sibling, at(z, x, yh, other), at(z, x, 1 - yh, other), at(z, x, 1 - yh, c))[i]
        return remote(
            modes.at[z_span(g), 0, 0, span], slab.at[z_span(g)], slab_s.at[g, i], slab_r.at[g], device
        )

    def fan_copy(g):
        return remote(slab.at[z_span(g)], slab.at[z_span(g)], slab_s.at[g, 0], slab_r.at[g], sibling)

    near = (1, 3, 2)

    def first(g):
        for d in near:
            start(x_first(g, d))
        start(y_first(g))

    def second(g):
        y_first(g).wait_recv()
        for d in near:
            start(x_second(g, d))
        for d in near:
            x_first(g, d).wait_recv()
        start(y_second(g))

    def take_z(g):
        begin, count, _ = GROUPS[g]
        for slot in range(begin, begin + count):
            if slot in (5, 6):
                z_pass(*((2, 1), (-2, -1))[slot - 5]).wait_recv()
            elif slot == 7:
                z_pass(2, 2).wait_recv()
                z_pass(-2, -2).wait_recv()
            elif slot > 0:
                z_push(-z_order[slot]).wait_recv()
        if g == 2:
            for j, hop in ((2, 1), (-2, -1)):
                start(z_pass(j, hop))
                start(z_pass(j, 2 * hop))

        @pl.when(source)
        def _():
            for i in (2, 1, 3, 0):
                slab_copy(g, i).start()

        first(g)

    def take_xy(s):
        for p, d in xy_order:
            if p == s:
                xy_push(s, d).wait_recv()
        for j in (2, 6, 1, 7):
            start(xy_then_z(s, j))

    def take_far(s):
        for j, hop in ((2, 1), (-2, -1)):
            xy_then_z(s, j).wait_recv()
            start(pass_z(s, j, hop))
            if (s == 0) == (j == 2):
                start(pass_z(s, j, 2 * hop))

    def take_relay(g):
        @pl.when(relay)
        def _():
            fan_copy(g).wait_recv()
            fan_copy(g).start()

    for j in (1, 7):
        start(z_push(j))
    for s, d in xy_order[:3]:
        start(xy_push(s, d))
    for j in (2, 6):
        start(z_push(j))
    for s, d in xy_order[3:]:
        start(xy_push(s, d))
    take_z(0)
    take_z(1)
    take_xy(0)
    take_z(2)
    take_xy(1)
    second(0)
    take_relay(0)
    take_z(3)
    second(1)
    take_relay(1)
    take_far(0)
    take_far(1)
    second(2)
    take_relay(2)
    second(3)
    take_relay(3)

    @pl.when(source)
    def _():
        slab[...] = modes[:, 0, 0, pl.ds(pl.multiple_of(32 * yh, 32), 32), :]

    @pl.when(leaf)
    def _():
        for g in range(len(GROUPS)):
            fan_copy(g).wait_recv()

    def slot_at(q):
        r = lax.rem(q - z + NZ, NZ)
        return jnp.where(r <= 4, 2 * r - (r > 0).astype(jnp.int32), 2 * (NZ - r))

    rows = slab.shape[1]
    wide = slab.shape[2]
    frames = NZ * wide
    edge = jnp.zeros((rows, 128), jnp.float32)
    line = jnp.concatenate([edge] + [slab[slot_at(i)].astype(jnp.float32) for i in range(NZ)] + [edge], axis=1)
    span = frames + 256
    lane = lax.broadcasted_iota(jnp.int32, (rows, wide), 1)
    for i in range(SHIFTS):
        d = i - HIST
        moved = line if d == 0 else pltpu.roll(line, (span - d) % span, 1)
        for q in range(NZ):
            piece = moved[:, 128 + q * wide : 128 + (q + 1) * wide]
            if q == NZ - 1:
                piece = jnp.where(lane <= wide - 1 - HIST + max(0, -d), piece, 0.0)
            left[q, i * rows : (i + 1) * rows, :] = piece.astype(jnp.bfloat16)
    a_edge[...] = line[:, frames : frames + 128]

    def block(slot):
        pieces = []
        for yh_ in range(2):
            for x_ in range(NX):
                s = lax.rem(yh + yh_, 2)
                r = lax.rem(x_ - x + NX, NX)
                pieces.append(modes[slot, s, r + (r == 2).astype(jnp.int32) - (r == 3).astype(jnp.int32)])
        return jnp.concatenate(pieces, axis=0)

    def dot(slot):
        return lax.dot_general(
            left[zs[z_order[slot]]], block(slot), (((1,), (1,)), ((), ())), preferred_element_type=jnp.float32
        ).reshape(sums.shape)

    for g, (begin, count, _) in enumerate(GROUPS):
        for d in near:
            x_second(g, d).wait_recv()
        y_second(g).wait_recv()
        value = None
        for slot in range(begin, begin + count):
            if z_order[slot] not in (0, 2, 6):
                for s in range(2):
                    xy_then_z(s, -z_order[slot]).wait_recv()
            value = dot(slot) if value is None else value + dot(slot)
        if g == 0:
            sums[...] = value
        else:
            sums[...] += value
    tail = block(slot_at(NZ - 1))[:, wide - 128 :].astype(jnp.float32)
    g_edge[...] = tail.T[120:128, :]

    for copy in sent:
        copy.wait_send()
    for k in range(NX):
        @pl.when(jnp.logical_not(jnp.logical_and(self_red, x == k)))
        def _():
            red_copy(k, c).wait_send()
    @pl.when(source)
    def _():
        for g in range(len(GROUPS)):
            for i in range(4):
                slab_copy(g, i).wait_send()

    @pl.when(relay)
    def _():
        for g in range(len(GROUPS)):
            fan_copy(g).wait_send()


def spread_kernel(scale, sums, a_edge, g_edge, out, stage, sem):
    copies = []
    for i in range(SHIFTS):
        d = i - HIST
        l1, l2 = (HIST - d, HIST) if d >= 0 else (HIST, HIST + d)
        value = sums[i]
        while True:
            stage[l1, l2] = value * scale
            copy = pltpu.make_async_copy(stage.at[l1, l2], out.at[l1, l2], sem.at[l1, l2])
            copy.start()
            copies.append(copy)
            if min(l1, l2) == 0:
                break
            l1, l2 = l1 - 1, l2 - 1
            value = value + a_edge[:, 127 - l1 : 128 - l1] * g_edge[7 - l2 : 8 - l2, :]
    for copy in copies:
        copy.wait()


def local(slopes, reconstructor):
    frames_dev, depth = slopes.shape
    block = reconstructor.shape[1]
    frames = frames_dev * NZ
    width = 2 * block
    rows = 32
    piece = block // NX
    vmem = pl.BlockSpec(memory_space=pltpu.VMEM)
    hbm = pl.BlockSpec(memory_space=pl.ANY)
    dma = pltpu.SemaphoreType.DMA
    sums, a_edge, g_edge = pl.pallas_call(
        gather_kernel,
        out_shape=[
            jax.ShapeDtypeStruct((SHIFTS, rows, width), jnp.float32),
            jax.ShapeDtypeStruct((rows, 128), jnp.float32),
            jax.ShapeDtypeStruct((8, width), jnp.float32),
        ],
        in_specs=[hbm, hbm],
        out_specs=[vmem, vmem, vmem],
        scratch_shapes=[
            pltpu.VMEM((frames_dev, depth), jnp.bfloat16),
            pltpu.VMEM((depth, block), jnp.bfloat16),
            pltpu.VMEM((NX, piece, frames_dev), jnp.float32),
            pltpu.VMEM((NC, piece, frames_dev), jnp.float32),
            pltpu.VMEM((NZ, 2, NX, piece, frames_dev), jnp.bfloat16),
            pltpu.VMEM((NZ, rows, frames_dev), jnp.bfloat16),
            pltpu.VMEM((NZ, SHIFTS * rows, frames_dev), jnp.bfloat16),
            dma((2, depth // CHUNK)),
            dma((NX,)), dma((NC,)),
            dma((4, 4)), dma((4,)),
            dma((2, NX)), dma((2, NX)),
            dma((NZ,)), dma((NZ,)),
            dma((2, NZ)), dma((2, NZ)),
            dma((4, NX)), dma((4, NX)), dma((4,)), dma((4,)),
            dma((4, NX)), dma((4, NX)), dma((4,)), dma((4,)),
        ],
        compiler_params=pltpu.CompilerParams(
            collective_id=0, has_side_effects=True, vmem_limit_bytes=51 * 2**20
        ),
        name="gather",
    )(slopes, reconstructor)
    scale = float(frames) ** -0.5
    out = pl.pallas_call(
        functools.partial(spread_kernel, scale),
        out_shape=jax.ShapeDtypeStruct((LAGS, LAGS, rows, width), jnp.float32),
        in_specs=[vmem, vmem, vmem],
        out_specs=pl.BlockSpec(memory_space=pl.ANY),
        scratch_shapes=[pltpu.VMEM((LAGS, LAGS, rows, width), jnp.float32), dma((LAGS, LAGS))],
        compiler_params=pltpu.CompilerParams(vmem_limit_bytes=32 * 2**20),
        name="spread",
    )(sums, a_edge, g_edge)
    return out.transpose(0, 2, 1, 3)


def solution(mesh):
    return jax.shard_map(
        local,
        mesh=mesh,
        in_specs=(P("tm", "col"), P("col", "row")),
        out_specs=P(None, ("tm", "row"), None, "col"),
        check_vma=False,
    )
```

```python
import functools

import jax
import jax.numpy as jnp
from jax import lax
from jax.experimental import pallas as pl
from jax.experimental.pallas import tpu as pltpu
from jax.sharding import PartitionSpec as P

MESH = pl.DeviceIdType.MESH
HIST = 5
LAGS = HIST + 1
SHIFTS = 2 * HIST + 1
NZ, NX, NC = 8, 4, 4
CHUNK = 1024
EARLY = 16
GROUPS = ((0, 1, 32), (1, 2, 32), (3, 2, 32), (5, 3, 32))


def gather_kernel(
    slopes_hbm, recon_hbm, sums, a_edge, g_edge,
    slopes, recon, part, inbox, modes, slab, left,
    load_sem, red_s, red_r, slab_s, slab_r,
    xy_s, xy_r, z_s, z_r, xyz_s, xyz_r, x1_s, x1_r, y1_s, y1_r, x2_s, x2_r, y2_s, y2_r,
):
    z = lax.axis_index("tm")
    row = lax.axis_index("row")
    c = lax.axis_index("col")
    x, yh = row // 2, row % 2
    yl, core = c // 2, c % 2
    depth = slopes_hbm.shape[1]
    chunks = depth // CHUNK

    def at(z_, x_, yh_, c_):
        return (z_, x_ * 2 + yh_, c_)

    loads = []
    for i in range(chunks):
        span = pl.ds(i * CHUNK, CHUNK)
        loads.append((
            pltpu.make_async_copy(slopes_hbm.at[:, span], slopes.at[:, span], load_sem.at[0, i]),
            pltpu.make_async_copy(recon_hbm.at[span], recon.at[span], load_sem.at[1, i]),
        ))
    for pair in loads:
        for copy in pair:
            copy.start()

    self_red = x == c
    source = jnp.logical_and(c == z // 2, yh == z % 2)
    relay = jnp.logical_and(core == (z // 2) % 2, jnp.logical_not(source))
    leaf = core != (z // 2) % 2
    zs = [(z + j) % NZ for j in range(NZ)]
    xs = [(x + j) % NX for j in range(NX)]
    yhs = (yh, 1 - yh)
    sibling = at(z, x, yh, 2 * yl + 1 - core)

    z_order = (0, 1, 7, 2, 6, 3, 5, 4)
    xy_order = ((0, 1), (0, 3), (0, 2), (1, 0), (1, 1), (1, 3), (1, 2))

    def z_peer(j):
        return at(zs[j], x, yh, c)

    def xy_peer(s, d):
        return at(z, xs[d], yhs[s], c)

    barrier = pltpu.get_barrier_semaphore()

    def greet(device):
        pl.semaphore_signal(barrier, inc=1, device_id=device, device_id_type=MESH)

    for s in range(NC):
        @pl.when(jnp.logical_not(jnp.logical_and(self_red, c == s)))
        def _():
            greet(at(z, c, yh, s))
    for s, d in xy_order:
        greet(xy_peer(s, d))
    for j in (1, 7, 2, 6):
        greet(z_peer(j))

    @pl.when(relay)
    def _():
        greet(at(z, x, z % 2, z // 2))

    @pl.when(leaf)
    def _():
        greet(sibling)

    total = jnp.zeros((slopes.shape[0], recon.shape[1]), jnp.float32)
    for i in range(chunks):
        for copy in loads[i]:
            copy.wait()
        total += jnp.dot(
            slopes[:, i * CHUNK : (i + 1) * CHUNK],
            recon[i * CHUNK : (i + 1) * CHUNK, :],
            preferred_element_type=jnp.float32,
        )
    part[...] = total.T.reshape(part.shape)

    expected = (
        15
        - self_red.astype(jnp.int32)
        + 4 * source.astype(jnp.int32)
        + relay.astype(jnp.int32)
    )
    pl.semaphore_wait(barrier, expected)

    def red_copy(d, slot):
        return pltpu.make_async_remote_copy(
            src_ref=part.at[xs[d]], dst_ref=inbox.at[slot], send_sem=red_s.at[d], recv_sem=red_r.at[slot],
            device_id=at(z, xs[d], yh, x), device_id_type=MESH,
        )

    for d in (2, 1, 3):
        red_copy(d, c).start()

    @pl.when(jnp.logical_not(self_red))
    def _():
        red_copy(0, c).start()

    @pl.when(self_red)
    def _():
        inbox[c] = part[x]

    for s in range(NC):
        @pl.when(jnp.logical_not(jnp.logical_and(self_red, c == s)))
        def _():
            red_copy(0, s).wait_recv()

    own = (inbox[0] + inbox[1]) + (inbox[2] + inbox[3])
    modes[0, 0, 0] = own.astype(jnp.bfloat16)

    def remote(src, dst, send, recv, device):
        return pltpu.make_async_remote_copy(
            src_ref=src, dst_ref=dst, send_sem=send, recv_sem=recv, device_id=device, device_id_type=MESH
        )

    sent = []

    def start(copy):
        copy.start()
        sent.append(copy)

    def x_slot(d):
        return (0, 1, 3, 2)[d % NX]

    def z_slot(j):
        return z_order.index(j % NZ)

    early, late = pl.ds(0, EARLY), pl.ds(EARLY, 64 - EARLY)

    def part_a(g):
        return pl.ds(EARLY, GROUPS[g][2])

    def part_b(g):
        return pl.ds(EARLY + GROUPS[g][2], 64 - EARLY - GROUPS[g][2])

    def z_span(g):
        return pl.ds(GROUPS[g][0], GROUPS[g][1])

    def xy_push(s, d):
        slot = x_slot(-d)
        return remote(
            modes.at[0, 0, 0, early], modes.at[0, s, slot, early], xy_s.at[s, slot], xy_r.at[s, slot], xy_peer(s, d)
        )

    def z_push(j):
        slot = z_slot(-j)
        return remote(modes.at[0, 0, 0], modes.at[slot, 0, 0], z_s.at[slot], z_r.at[slot], z_peer(j))

    def z_pass(j, hops):
        slot = z_slot(-j - hops)
        sem, rows_ = slot, pl.ds(0, 64)
        if abs(hops) == 2:
            sem, rows_ = (slot, pl.ds(0, 32)) if hops > 0 else (0, pl.ds(32, 32))
        return remote(
            modes.at[z_slot(-j), 0, 0, rows_], modes.at[slot, 0, 0, rows_], z_s.at[sem], z_r.at[sem],
            z_peer(hops % NZ),
        )

    def slots(s):
        return pl.ds(1 - s, NX - 1 + s)

    def xy_then_z(s, j):
        slot = z_slot(-j)
        return remote(
            modes.at[0, s, slots(s), early], modes.at[slot, s, slots(s), early], xyz_s.at[s, slot], xyz_r.at[s, slot],
            z_peer(j),
        )

    def pass_z(s, j, hops):
        slot = z_slot(-j - hops)
        return remote(
            modes.at[z_slot(-j), s, slots(s), early], modes.at[slot, s, slots(s), early],
            xyz_s.at[s, slot], xyz_r.at[s, slot], z_peer(hops % NZ),
        )

    def x_first(g, d):
        slot = x_slot(-d)
        return remote(
            modes.at[z_span(g), 0, 0, late], modes.at[z_span(g), 0, slot, late], x1_s.at[g, slot], x1_r.at[g, slot],
            xy_peer(0, d),
        )

    def y_first(g):
        return remote(
            modes.at[z_span(g), 0, 0, late], modes.at[z_span(g), 1, 0, late], y1_s.at[g], y1_r.at[g], xy_peer(1, 0)
        )

    def x_second(g, d):
        slot = x_slot(-d)
        return remote(
            modes.at[z_span(g), 1, 0, part_a(g)], modes.at[z_span(g), 1, slot, part_a(g)],
            x2_s.at[g, slot], x2_r.at[g, slot], xy_peer(0, d),
        )

    def y_second(g):
        span = pl.ds(1, NX - 1)
        return remote(
            modes.at[z_span(g), 0, span, part_b(g)], modes.at[z_span(g), 1, span, part_b(g)],
            y2_s.at[g], y2_r.at[g], xy_peer(1, 0),
        )

    def slab_copy(g, i):
        plane = yh if i < 2 else 1 - yh
        span = pl.ds(pl.multiple_of(32 * plane, 32), 32)
        other = 2 * (1 - yl) + core
        device = (sibling, at(z, x, yh, other), at(z, x, 1 - yh, other), at(z, x, 1 - yh, c))[i]
        return remote(
            modes.at[z_span(g), 0, 0, span], slab.at[z_span(g)], slab_s.at[g, i], slab_r.at[g], device
        )

    def fan_copy(g):
        return remote(slab.at[z_span(g)], slab.at[z_span(g)], slab_s.at[g, 0], slab_r.at[g], sibling)

    near = (2, 1, 3)

    def first(g):
        for d in near:
            start(x_first(g, d))
        start(y_first(g))

    def second(g):
        y_first(g).wait_recv()
        for d in near:
            start(x_second(g, d))
        for d in near:
            x_first(g, d).wait_recv()
        start(y_second(g))

    def take_z(g):
        begin, count, _ = GROUPS[g]
        for slot in range(begin, begin + count):
            if slot in (5, 6):
                z_pass(*((2, 1), (-2, -1))[slot - 5]).wait_recv()
            elif slot == 7:
                z_pass(2, 2).wait_recv()
                z_pass(-2, -2).wait_recv()
            elif slot > 0:
                z_push(-z_order[slot]).wait_recv()
        if g == 2:
            for j, hop in ((2, 1), (-2, -1)):
                start(z_pass(j, hop))
                start(z_pass(j, 2 * hop))

        @pl.when(source)
        def _():
            for i in (2, 1, 3, 0):
                slab_copy(g, i).start()

        first(g)

    def take_xy(s):
        for p, d in xy_order:
            if p == s:
                xy_push(s, d).wait_recv()
        for j in (2, 6, 1, 7):
            start(xy_then_z(s, j))

    def take_far(s):
        for j, hop in ((2, 1), (-2, -1)):
            xy_then_z(s, j).wait_recv()
            start(pass_z(s, j, hop))
            if (s == 0) == (j == 2):
                start(pass_z(s, j, 2 * hop))

    def take_relay(g):
        @pl.when(relay)
        def _():
            fan_copy(g).wait_recv()
            fan_copy(g).start()

    for j in (1, 7):
        start(z_push(j))
    for s, d in xy_order[:3]:
        start(xy_push(s, d))
    for j in (2, 6):
        start(z_push(j))
    for s, d in xy_order[3:]:
        start(xy_push(s, d))
    take_z(0)
    take_z(1)
    take_xy(0)
    take_z(2)
    take_xy(1)
    second(0)
    take_z(3)
    second(1)
    second(2)
    take_far(0)
    take_far(1)
    second(3)
    for g in range(len(GROUPS)):
        take_relay(g)

    @pl.when(source)
    def _():
        slab[...] = modes[:, 0, 0, pl.ds(pl.multiple_of(32 * yh, 32), 32), :]

    @pl.when(leaf)
    def _():
        for g in range(len(GROUPS)):
            fan_copy(g).wait_recv()

    def slot_at(q):
        r = lax.rem(q - z + NZ, NZ)
        return jnp.where(r <= 4, 2 * r - (r > 0).astype(jnp.int32), 2 * (NZ - r))

    rows = slab.shape[1]
    wide = slab.shape[2]
    frames = NZ * wide
    edge = jnp.zeros((rows, 128), jnp.float32)
    line = jnp.concatenate([edge] + [slab[slot_at(i)].astype(jnp.float32) for i in range(NZ)] + [edge], axis=1)
    span = frames + 256
    lane = lax.broadcasted_iota(jnp.int32, (rows, wide), 1)
    for i in range(SHIFTS):
        d = i - HIST
        moved = line if d == 0 else pltpu.roll(line, (span - d) % span, 1)
        for q in range(NZ):
            piece = moved[:, 128 + q * wide : 128 + (q + 1) * wide]
            if q == NZ - 1:
                piece = jnp.where(lane <= wide - 1 - HIST + max(0, -d), piece, 0.0)
            left[q, i * rows : (i + 1) * rows, :] = piece.astype(jnp.bfloat16)
    a_edge[...] = line[:, frames : frames + 128]

    def block(slot):
        pieces = []
        for yh_ in range(2):
            for x_ in range(NX):
                s = lax.rem(yh + yh_, 2)
                r = lax.rem(x_ - x + NX, NX)
                pieces.append(modes[slot, s, r + (r == 2).astype(jnp.int32) - (r == 3).astype(jnp.int32)])
        return jnp.concatenate(pieces, axis=0)

    def dot(slot):
        return lax.dot_general(
            left[zs[z_order[slot]]], block(slot), (((1,), (1,)), ((), ())), preferred_element_type=jnp.float32
        ).reshape(sums.shape)

    for g, (begin, count, _) in enumerate(GROUPS):
        for d in near:
            x_second(g, d).wait_recv()
        y_second(g).wait_recv()
        value = None
        for slot in range(begin, begin + count):
            if z_order[slot] not in (0, 2, 6):
                for s in range(2):
                    xy_then_z(s, -z_order[slot]).wait_recv()
            value = dot(slot) if value is None else value + dot(slot)
        if g == 0:
            sums[...] = value
        else:
            sums[...] += value
    tail = block(slot_at(NZ - 1))[:, wide - 128 :].astype(jnp.float32)
    g_edge[...] = tail.T[120:128, :]

    for copy in sent:
        copy.wait_send()
    for d in (1, 2, 3):
        red_copy(d, c).wait_send()

    @pl.when(jnp.logical_not(self_red))
    def _():
        red_copy(0, c).wait_send()

    @pl.when(source)
    def _():
        for g in range(len(GROUPS)):
            for i in range(4):
                slab_copy(g, i).wait_send()

    @pl.when(relay)
    def _():
        for g in range(len(GROUPS)):
            fan_copy(g).wait_send()


def spread_kernel(scale, sums, a_edge, g_edge, out, stage, sem):
    copies = []
    for i in range(SHIFTS):
        d = i - HIST
        l1, l2 = (HIST - d, HIST) if d >= 0 else (HIST, HIST + d)
        value = sums[i]
        while True:
            stage[l1, l2] = value * scale
            copy = pltpu.make_async_copy(stage.at[l1, l2], out.at[l1, l2], sem.at[l1, l2])
            copy.start()
            copies.append(copy)
            if min(l1, l2) == 0:
                break
            l1, l2 = l1 - 1, l2 - 1
            value = value + a_edge[:, 127 - l1 : 128 - l1] * g_edge[7 - l2 : 8 - l2, :]
    for copy in copies:
        copy.wait()


def local(slopes, reconstructor):
    frames_dev, depth = slopes.shape
    block = reconstructor.shape[1]
    frames = frames_dev * NZ
    width = 2 * block
    rows = 32
    piece = block // NX
    vmem = pl.BlockSpec(memory_space=pltpu.VMEM)
    hbm = pl.BlockSpec(memory_space=pl.ANY)
    dma = pltpu.SemaphoreType.DMA
    sums, a_edge, g_edge = pl.pallas_call(
        gather_kernel,
        out_shape=[
            jax.ShapeDtypeStruct((SHIFTS, rows, width), jnp.float32),
            jax.ShapeDtypeStruct((rows, 128), jnp.float32),
            jax.ShapeDtypeStruct((8, width), jnp.float32),
        ],
        in_specs=[hbm, hbm],
        out_specs=[vmem, vmem, vmem],
        scratch_shapes=[
            pltpu.VMEM((frames_dev, depth), jnp.bfloat16),
            pltpu.VMEM((depth, block), jnp.bfloat16),
            pltpu.VMEM((NX, piece, frames_dev), jnp.float32),
            pltpu.VMEM((NC, piece, frames_dev), jnp.float32),
            pltpu.VMEM((NZ, 2, NX, piece, frames_dev), jnp.bfloat16),
            pltpu.VMEM((NZ, rows, frames_dev), jnp.bfloat16),
            pltpu.VMEM((NZ, SHIFTS * rows, frames_dev), jnp.bfloat16),
            dma((2, depth // CHUNK)),
            dma((NX,)), dma((NC,)),
            dma((4, 4)), dma((4,)),
            dma((2, NX)), dma((2, NX)),
            dma((NZ,)), dma((NZ,)),
            dma((2, NZ)), dma((2, NZ)),
            dma((4, NX)), dma((4, NX)), dma((4,)), dma((4,)),
            dma((4, NX)), dma((4, NX)), dma((4,)), dma((4,)),
        ],
        compiler_params=pltpu.CompilerParams(
            collective_id=0, has_side_effects=True, vmem_limit_bytes=51 * 2**20
        ),
        name="gather",
    )(slopes, reconstructor)
    scale = float(frames) ** -0.5
    out = pl.pallas_call(
        functools.partial(spread_kernel, scale),
        out_shape=jax.ShapeDtypeStruct((LAGS, LAGS, rows, width), jnp.float32),
        in_specs=[vmem, vmem, vmem],
        out_specs=pl.BlockSpec(memory_space=pl.ANY),
        scratch_shapes=[pltpu.VMEM((LAGS, LAGS, rows, width), jnp.float32), dma((LAGS, LAGS))],
        compiler_params=pltpu.CompilerParams(vmem_limit_bytes=32 * 2**20),
        name="spread",
    )(sums, a_edge, g_edge)
    return out.transpose(0, 2, 1, 3)


def solution(mesh):
    return jax.shard_map(
        local,
        mesh=mesh,
        in_specs=(P("tm", "col"), P("col", "row")),
        out_specs=P(None, ("tm", "row"), None, "col"),
        check_vma=False,
    )
```
